128 devices in a mesh: island: 2 (over y_lo), fsdp: 64 (over z, x, y_hi, core).
Axes of the slice: x: 4, y: 4 (y_hi: 2, y_lo: 2; y = y_hi * 2 + y_lo), z: 4, core: 2. Of those that a mesh axis runs over, the one named last changes fastest.
Arguments:
- inner_params: float32 [2, 3, 3584, 3584], P('island', None, 'fsdp'), may hold values from -0.09375 to 0.09375
- inner_grads: bfloat16 [2, 3, 3584, 3584], P('island', None, 'fsdp'), may hold values from -6 to 6
- adam_first: float32 [2, 3, 3584, 3584], P('island', None, 'fsdp'), may hold values from -0.6 to 0.6
- adam_second: float32 [2, 3, 3584, 3584], P('island', None, 'fsdp'), may hold values from 0.0001 to 0.01
- anchor: float32 [3584, 3584], P('fsdp'), may hold values from -0.09375 to 0.09375
- momentum: float32 [3584, 3584], P('fsdp'), may hold values from -0.046875 to 0.046875
- tokens: bfloat16 [65536, 3584], P(('island', 'fsdp')), may hold values from -6 to 6
- frag_index: int32 [1], replicated, may hold values from 0 to 99999
- plan: int32 [3], replicated, may hold values from 0 to 2, each once
Outputs:
- params_out: float32 [2, 3, 3584, 3584], P('island', None, 'fsdp')
- first_out: float32 [2, 3, 3584, 3584], P('island', None, 'fsdp')
- second_out: float32 [2, 3, 3584, 3584], P('island', None, 'fsdp')
- momentum_out: float32 [3584, 3584], P('fsdp')
- projected: bfloat16 [65536, 3584], P(('island', 'fsdp'))
The draws below stay inside these ranges and needn't reach their ends.
Inputs may be any that keep to these rules, and one draw needn't show every extreme that they name: `plan`: each fragment number names exactly one layer.
All inputs are finite; a program needn't handle non-finite values.
Results may differ from the reference program's by a relative error of at most 0.0065.
Values may be sent and summed in bfloat16 or wider, within the bound.
No kernel may reach another device: no remote copies, remote signals or barrier semaphores. Data moves between devices by JAX's collectives and lax.ppermute only.
A program may use at most 192 MiB of HBM per device.

```python
import math
import jax
import jax.numpy as jnp
from jax import lax

DIN = 3584
DOUT = 3584
LAYERS = 3
STEP = 40
TOKENS = 65536
N_ISLAND = 2


def steps_of(rng, dims, shards, least, high):
    factor_of, own = 1.0, jax.random.fold_in(rng, 6)
    for axis_at, shards_of in shards:
        steps = jnp.exp(jax.random.uniform(jax.random.fold_in(own, axis_at), (shards_of,), jnp.float32, least / len(shards), high / len(shards)))
        factor_of = factor_of * jnp.repeat(steps, dims[axis_at] // shards_of).reshape([-1 if axis == axis_at else 1 for axis in range(len(dims))])
    return factor_of


def centred(own_key, dims, spread, limit, cuts=(), kind=jnp.bfloat16):
    result = spread * jax.random.normal(own_key, dims, jnp.float32)
    if cuts:
        result = result * steps_of(own_key, dims, cuts, -0.22, 0.18)
    return jnp.clip(result, -limit, limit).astype(kind)


def setup_inputs(seed: int = 0) -> dict:
    key_list = jax.random.split(jax.random.key(seed), 10)
    return {
        "inner_params": centred(key_list[0], (N_ISLAND, LAYERS, DIN, DOUT), DIN ** -0.5, 0.09375, ((0, 2), (2, 64)), jnp.float32),
        "inner_grads": centred(key_list[1], (N_ISLAND, LAYERS, DIN, DOUT), 1.0, 6.0, ((0, 2), (2, 64))),
        "adam_first": centred(key_list[2], (N_ISLAND, LAYERS, DIN, DOUT), 0.1, 0.6, ((0, 2), (2, 64)), jnp.float32),
        "adam_second": jnp.clip(jnp.exp(math.log(0.01) - 4.6051702 * jax.random.uniform(key_list[3], (N_ISLAND, LAYERS, DIN, DOUT), jnp.float32) ** steps_of(key_list[3], (N_ISLAND, LAYERS, DIN, DOUT), ((0, 2), (2, 64)), -0.2, 0.2)), 0.0001, 0.01),
        "anchor": centred(key_list[4], (DIN, DOUT), DIN ** -0.5, 0.09375, ((0, 64),), jnp.float32),
        "momentum": centred(key_list[5], (DIN, DOUT), (DIN * 4) ** -0.5, 0.046875, ((0, 64),), jnp.float32),
        "tokens": centred(key_list[6], (TOKENS, DIN), 1.0, 6.0, ((0, 128),)),
        "frag_index": jax.random.randint(key_list[7], (1,), 0, 100000).astype(jnp.int32),
        "plan": jax.random.permutation(key_list[8], LAYERS).astype(jnp.int32),
    }


outer_rate = 0.7
outer_mu = 0.9
inner_rate = 0.01
decay_rate = 0.1
beta_one = 0.9
beta_two = 0.95
adam_eps = 1e-08

def adamw_step(params, grads, first, second):
    grad_f = grads.astype(jnp.float32)
    first_new = beta_one * first + (1.0 - beta_one) * grad_f
    second_new = beta_two * second + (1.0 - beta_two) * grad_f * grad_f
    first_hat = first_new / (1.0 - beta_one ** STEP)
    second_hat = second_new / (1.0 - beta_two ** STEP)
    stepped = params * (1.0 - inner_rate * decay_rate) - inner_rate * first_hat / (jnp.sqrt(second_hat) + adam_eps)
    return (stepped, first_new, second_new)

def reference(inner_params, inner_grads, adam_first, adam_second, anchor, momentum, tokens, frag_index, plan):
    layer_ids = jnp.arange(LAYERS, dtype=jnp.int32)
    current = (frag_index[0] % LAYERS).astype(jnp.int32)
    chosen = jnp.sum(jnp.where(plan == current, layer_ids, 0)).astype(jnp.int32)
    drifted = lax.dynamic_index_in_dim(inner_params, chosen, 1, keepdims=False)
    pseudo_grad = lax.optimization_barrier(jnp.sum(anchor[None] - drifted, axis=0)) / N_ISLAND
    momentum_out = outer_mu * momentum + pseudo_grad
    new_anchor = anchor - outer_rate * (pseudo_grad + outer_mu * momentum_out)
    stepped, first_new, second_new = adamw_step(inner_params, inner_grads, adam_first, adam_second)
    is_frag = (layer_ids == chosen)[None, :, None, None]
    params_out = jnp.where(is_frag, new_anchor[None, None], stepped)
    first_out = jnp.where(is_frag, adam_first, first_new)
    second_out = jnp.where(is_frag, adam_second, second_new)
    weight_bf = new_anchor.astype(jnp.bfloat16)
    projected = jnp.dot(tokens, weight_bf, preferred_element_type=jnp.float32).astype(jnp.bfloat16)
    return (params_out, first_out, second_out, momentum_out, projected)
```

```python
import functools

import jax
import jax.numpy as jnp
import numpy as np
from jax import lax
from jax.experimental import pallas as pl
from jax.experimental.pallas import tpu as pltpu
from jax.sharding import Mesh
from jax.sharding import PartitionSpec as P

STEP = 40
LAYERS = 3
outer_rate = 0.7
outer_mu = 0.9
inner_rate = 0.01
decay_rate = 0.1
beta_one = 0.9
beta_two = 0.95
adam_eps = 1e-08

ROWS = 56
CHIP = 2 * ROWS
D = 3584
HALF = D // 2
PART = 768
SIDE = 256
GROUP = 256
GROUPS = 3
SENT = PART + SIDE
TOK = 512

ALL = ("yl", "z", "x", "yh", "core")
CHIPS = ("z", "x", "yh")
FLIPS = (("x", 1), ("y", 1), ("z", 1), ("x", 3), ("y", 3), ("z", 3))


def order(group, core):
    s = (group + 3 * core) % 6
    return FLIPS[s:] + FLIPS[:s]


def flipped(i, flip):
    core, yh, x, z, yl = i % 2, i // 2 % 2, i // 4 % 4, i // 16 % 4, i // 64
    y = yh * 2 + yl
    axis, mask = flip
    x, y, z = (v ^ mask if name == axis else v for name, v in (("x", x), ("y", y), ("z", z)))
    return ((y % 2 * 4 + z) * 4 + x) * 4 + y // 2 * 2 + core


def exchange(value, group, step):
    flips = [order(group, core)[step] for core in (0, 1)]
    return lax.ppermute(value, ALL, [(i, flipped(i, flips[i % 2])) for i in range(128)])


def code_masks(group, core):
    shift = {"z": 4, "x": 2, "y": 0}
    bits = [mask << shift[axis] for axis, mask in order(group, core)]
    return [functools.reduce(lambda a, b: a ^ b, [bits[k] for k in range(6) if r >> k & 1], 0) for r in range(64)]


def swap_cores(value):
    return lax.ppermute(value, "core", [(0, 1), (1, 0)])


def chosen_of(frag_ref, plan_ref):
    current = lax.rem(frag_ref[0], LAYERS)
    return jnp.where(plan_ref[0] == current, 0, jnp.where(plan_ref[1] == current, 1, 2))


def lanes(start, size):
    return pl.ds(pl.multiple_of(start, 128), size)


def outer(anchor, momentum, summed):
    pseudo = summed * 0.5
    momentum_new = outer_mu * momentum + pseudo
    return anchor - outer_rate * (pseudo + outer_mu * momentum_new), momentum_new


def diff_kernel(frag_ref, plan_ref, anchor_ref, params_ref, diff_ref, sent_ref):
    other = 1 - lax.axis_index("yl")
    diff_ref[...] = anchor_ref[...] - params_ref[0, 0]
    for half in (0, 1):
        at = half * SENT
        sent_ref[:, at : at + PART] = diff_ref[:, lanes(half * HALF + other * PART, PART)].astype(jnp.bfloat16)
        side = half * HALF + 2 * PART
        sent_ref[:, at + PART : at + SENT] = diff_ref[:, side : side + SIDE].astype(jnp.bfloat16)


def weight_kernel(anchor_ref, momentum_ref, diff_ref, received_ref, keep_ref, give_ref):
    island, core = lax.axis_index("yl"), lax.axis_index("core")
    for out_ref, half in ((keep_ref, core), (give_ref, 1 - core)):
        for at, src, size in (
            (0, half * HALF + island * PART, PART),
            (PART, half * HALF + 2 * PART, SIDE),
        ):
            cols = lanes(src, size)
            got = received_ref[:, lanes(half * SENT + at, size)].astype(jnp.float32)
            new, _ = outer(anchor_ref[:, cols], momentum_ref[:, cols], diff_ref[:, cols] + got)
            out_ref[:, at : at + size] = new


def join_kernel(keep_ref, got_ref, *refs):
    outs, rows_ref = refs[:-1], refs[-1]
    core = lax.axis_index("core")
    rows_ref[pl.ds(pl.multiple_of(core * ROWS, 8), ROWS), :] = keep_ref[...]
    rows_ref[pl.ds(pl.multiple_of((1 - core) * ROWS, 8), ROWS), :] = got_ref[...]
    for i, out_ref in enumerate(outs):
        out_ref[0] = rows_ref[:, i * GROUP : (i + 1) * GROUP].astype(jnp.bfloat16)


def adam_kernel(frag_ref, plan_ref, p_ref, g_ref, m_ref, v_ref, p_out, m_out, v_out):
    chosen = chosen_of(frag_ref, plan_ref)
    frozen = pl.program_id(0) == chosen

    @pl.when(frozen)
    def _():
        p_out[...] = p_ref[...]
        m_out[...] = m_ref[...]
        v_out[...] = v_ref[...]

    @pl.when(jnp.logical_not(frozen))
    def _():
        grad = g_ref[...].astype(jnp.float32)
        first = beta_one * m_ref[...] + (1.0 - beta_one) * grad
        second = beta_two * v_ref[...] + (1.0 - beta_two) * grad * grad
        first_hat = first * (1.0 / (1.0 - beta_one**STEP))
        second_hat = second * (1.0 / (1.0 - beta_two**STEP))
        p_out[...] = p_ref[...] * (1.0 - inner_rate * decay_rate) - inner_rate * first_hat / (
            jnp.sqrt(second_hat) + adam_eps
        )
        m_out[...] = first
        v_out[...] = second


def outer_kernel(frag_ref, plan_ref, anchor_ref, momentum_ref, diff_ref, got_ref, held_ref, momentum_out, p_out):
    new, momentum_new = outer(anchor_ref[...], momentum_ref[...], diff_ref[...] + got_ref[...])
    momentum_out[...] = momentum_new
    p_out[0, 0] = new


TILE = 256


def result_columns(group, half):
    return [half * HALF + group * GROUP, half * HALF + PART + group * GROUP]


def multiply(step, mine_ref, theirs_ref, weight, out_ref, result_ref, staged, sem, columns):
    n = TOK // TILE

    @pl.when(step < n)
    def _():
        out_ref[...] = jnp.dot(theirs_ref[...], weight(), preferred_element_type=jnp.float32).astype(jnp.bfloat16)

    @pl.when(step >= n)
    def _():
        staged[...] = jnp.dot(mine_ref[...], weight(), preferred_element_type=jnp.float32).astype(jnp.bfloat16)
        rows = pl.ds(pl.multiple_of((step - n) * TILE, TILE), TILE)
        copies = [
            pltpu.make_async_copy(
                staged.at[:, i * GROUP : (i + 1) * GROUP], result_ref.at[rows, lanes(at, GROUP)], sem.at[i]
            )
            for i, at in enumerate(columns)
        ]
        for copy in copies:
            copy.start()
        for copy in copies:
            copy.wait()


def group_kernel(group, has_buffer, mine_ref, theirs_ref, *refs):
    pieces, refs = refs[:4], refs[4 + has_buffer :]
    result_ref, out_ref, weight, staged, sem, load_sem = refs
    step = pl.program_id(0)
    core = lax.axis_index("core")

    @pl.when(step == 0)
    def _():
        here = lax.axis_index("z") * 16 + lax.axis_index("x") * 4 + lax.axis_index("yh") * 2 + lax.axis_index("yl")
        masks = [code_masks(group, c) for c in (0, 1)]
        for r in range(64):
            code = here ^ jnp.where(core == 0, masks[0][r], masks[1][r])
            pltpu.make_async_copy(
                pieces[r // 16].at[r % 16],
                weight.at[code // 2, :, lanes(code % 2 * GROUP, GROUP)],
                load_sem,
            ).start()
        pltpu.make_async_copy(weight, weight, load_sem).wait()

    multiply(
        step, mine_ref, theirs_ref, lambda: weight[...].reshape(D, 2 * GROUP),
        out_ref, result_ref, staged, sem, result_columns(group, core),
    )


def side_kernel(mine_ref, theirs_ref, weight_ref, result_ref, out_ref, staged, sem):
    core = lax.axis_index("core")
    multiply(
        pl.program_id(0), mine_ref, theirs_ref, lambda: weight_ref[...],
        out_ref, result_ref, staged, sem, [core * HALF + 2 * PART],
    )


def place_kernel(buffer_ref, *refs):
    received, result_ref, sem = refs[:-2], refs[-2], refs[-1]
    half = 1 - lax.axis_index("core")
    copies = []
    for group, got in enumerate(received):
        columns = result_columns(group, half) if group < GROUPS else [half * HALF + 2 * PART]
        for i, at in enumerate(columns):
            copies.append(
                pltpu.make_async_copy(
                    got.at[:, i * GROUP : (i + 1) * GROUP], result_ref.at[:, lanes(at, GROUP)], sem.at[len(copies)]
                )
            )
    for copy in copies:
        copy.start()
    for copy in copies:
        copy.wait()


ANY = pl.BlockSpec(memory_space=pl.ANY)
VMEM = pl.BlockSpec(memory_space=pltpu.VMEM)
LIMIT = pltpu.CompilerParams(vmem_limit_bytes=48 * 2**20)


def shape(dims, dtype):
    return jax.ShapeDtypeStruct(dims, dtype)


def cost(flops, moved):
    return pl.CostEstimate(flops=flops, bytes_accessed=moved, transcendentals=0)


def token_specs():
    n = TOK // TILE
    return [
        pl.BlockSpec((TILE, D), lambda i: (jnp.maximum(i - n, 0), 0)),
        pl.BlockSpec((TILE, D), lambda i: (jnp.minimum(i, n - 1), 0)),
    ]


def multiply_call(kernel, extra, extra_specs, tokens, others, width, scratch, buffer):
    n = TOK // TILE
    args = [tokens, others, *extra] + ([] if buffer is None else [buffer])
    return pl.pallas_call(
        kernel,
        grid=(2 * n,),
        in_specs=token_specs() + extra_specs + ([] if buffer is None else [ANY]),
        out_specs=[ANY, pl.BlockSpec((TILE, width), lambda i: (jnp.minimum(i, n - 1), 0))],
        out_shape=[shape((TOK, D), jnp.bfloat16), shape((TOK, width), jnp.bfloat16)],
        scratch_shapes=scratch + [
            pltpu.VMEM((TILE, width), jnp.bfloat16),
            pltpu.SemaphoreType.DMA((width // GROUP,)),
        ] + ([pltpu.SemaphoreType.DMA] if scratch else []),
        input_output_aliases={} if buffer is None else {len(args) - 1: 0},
        compiler_params=LIMIT,
        cost_estimate=cost(2 * 2 * TOK * D * width, 4 * TOK * D + 2 * D * width),
    )(*args)


def body(inner_params, inner_grads, adam_first, adam_second, anchor, momentum, tokens, frag_index, plan):
    f32, bf16 = jnp.float32, jnp.bfloat16
    others = swap_cores(tokens)

    def layer(i, frag_ref, plan_ref):
        return (0, chosen_of(frag_ref, plan_ref), 0, 0)

    def whole(i, frag_ref, plan_ref):
        return (0, 0)

    block = pl.BlockSpec((ROWS, D), whole)
    diff, sent = pl.pallas_call(
        diff_kernel,
        grid_spec=pltpu.PrefetchScalarGridSpec(
            num_scalar_prefetch=2,
            grid=(1,),
            in_specs=[block, pl.BlockSpec((1, 1, ROWS, D), layer)],
            out_specs=[block, pl.BlockSpec((ROWS, 2 * SENT), whole)],
        ),
        out_shape=[shape((ROWS, D), f32), shape((ROWS, 2 * SENT), bf16)],
        compiler_params=LIMIT,
    )(frag_index, plan, anchor, inner_params)
    islands = [(0, 1), (1, 0)]
    received = lax.ppermute(sent, "yl", islands)
    keep, give = pl.pallas_call(
        weight_kernel,
        in_specs=[VMEM] * 4,
        out_specs=[VMEM] * 2,
        out_shape=[shape((ROWS, SENT), f32)] * 2,
        compiler_params=LIMIT,
    )(anchor, momentum, diff, received)
    got = swap_cores(give)
    *cur, side = pl.pallas_call(
        join_kernel,
        in_specs=[VMEM] * 2,
        out_specs=[VMEM] * (GROUPS + 1),
        out_shape=[shape((1, CHIP, GROUP), bf16)] * (GROUPS + 1),
        scratch_shapes=[pltpu.VMEM((CHIP, SENT), f32)],
        compiler_params=LIMIT,
    )(keep, got)

    side_weight = lax.all_gather(side[0], CHIPS, axis=0, tiled=True)
    for step in range(4):
        arrived = [exchange(cur[q], q, step) for q in range(GROUPS)]
        cur = [jnp.concatenate([cur[q], arrived[q]], axis=0) for q in range(GROUPS)]
    fifth = [exchange(cur[q], q, 4) for q in range(GROUPS)]
    sixth = [exchange(cur[q], q, 5) for q in range(GROUPS)]
    last = [exchange(fifth[q], q, 5) for q in range(GROUPS)]

    width = 896
    stepped = pl.BlockSpec((1, 1, ROWS, width), lambda i, j, *_: (0, i, 0, j))
    state = shape((1, LAYERS, ROWS, D), f32)
    params_held, first_out, second_out = pl.pallas_call(
        adam_kernel,
        grid_spec=pltpu.PrefetchScalarGridSpec(
            num_scalar_prefetch=2,
            grid=(LAYERS, pl.cdiv(D, width)),
            in_specs=[stepped] * 4,
            out_specs=[stepped] * 3,
        ),
        out_shape=[state] * 3,
        compiler_params=LIMIT,
        cost_estimate=cost(20 * LAYERS * ROWS * D, 26 * LAYERS * ROWS * D),
    )(frag_index, plan, inner_params, inner_grads, adam_first, adam_second)

    diff_other = lax.ppermute(diff, "yl", islands)
    momentum_out, params_out = pl.pallas_call(
        outer_kernel,
        grid_spec=pltpu.PrefetchScalarGridSpec(
            num_scalar_prefetch=2,
            grid=(1,),
            in_specs=[block] * 4 + [ANY],
            out_specs=[block, pl.BlockSpec((1, 1, ROWS, D), layer)],
        ),
        out_shape=[shape((ROWS, D), f32), state],
        input_output_aliases={6: 1},
        compiler_params=LIMIT,
    )(frag_index, plan, anchor, momentum, diff, diff_other, params_held)

    result, out = multiply_call(side_kernel, [side_weight], [VMEM], tokens, others, SIDE, [], None)
    swapped = [swap_cores(out)]
    for q in range(GROUPS):
        result, out = multiply_call(
            functools.partial(group_kernel, q, 1), [cur[q], fifth[q], sixth[q], last[q]], [ANY] * 4, tokens, others,
            2 * GROUP, [pltpu.VMEM((D // CHIP, CHIP, 2 * GROUP), bf16)], result,
        )
        swapped.insert(q, swap_cores(out))
    projected = pl.pallas_call(
        place_kernel,
        in_specs=[ANY] * (GROUPS + 2),
        out_specs=ANY,
        out_shape=shape((TOK, D), bf16),
        scratch_shapes=[pltpu.SemaphoreType.DMA((2 * GROUPS + 1,))],
        input_output_aliases={0: 0},
        compiler_params=LIMIT,
    )(result, *swapped)
    return (params_out, first_out, second_out, momentum_out, projected)


def solution(mesh):
    torus = Mesh(np.asarray(mesh.devices).reshape(2, 4, 4, 2, 2), ALL)
    fsdp = ("z", "x", "yh", "core")
    state = P("yl", None, fsdp, None)
    rows = P(fsdp, None)
    tokens = P(ALL, None)
    return jax.shard_map(
        body,
        mesh=torus,
        in_specs=(state, state, state, state, rows, rows, tokens, P(), P()),
        out_specs=(state, state, state, rows, tokens),
        check_vma=False,
    )
```

```python
import functools

import jax
import jax.numpy as jnp
import numpy as np
from jax import lax
from jax.experimental import pallas as pl
from jax.experimental.pallas import tpu as pltpu
from jax.sharding import Mesh
from jax.sharding import PartitionSpec as P

STEP = 40
LAYERS = 3
outer_rate = 0.7
outer_mu = 0.9
inner_rate = 0.01
decay_rate = 0.1
beta_one = 0.9
beta_two = 0.95
adam_eps = 1e-08

ROWS = 56
CHIP = 2 * ROWS
D = 3584
HALF = D // 2
PART = HALF // 2
TILE = 128
GROUPS = 3
SHARE = (48, 32, 32)
ROOM = max(SHARE)
TOK = 512

ALL = ("yl", "z", "x", "yh", "core")
CHIPS = ("z", "x", "yh")
FLIPS = (("x", 1), ("y", 1), ("z", 1), ("x", 3), ("y", 3), ("z", 3))


def order(group, core):
    s = (group + 3 * core) % 6
    return FLIPS[s:] + FLIPS[:s]


def flipped(i, flip):
    core, yh, x, z, yl = i % 2, i // 2 % 2, i // 4 % 4, i // 16 % 4, i // 64
    y = yh * 2 + yl
    axis, mask = flip
    x, y, z = (v ^ mask if name == axis else v for name, v in (("x", x), ("y", y), ("z", z)))
    return ((y % 2 * 4 + z) * 4 + x) * 4 + y // 2 * 2 + core


def exchange(value, group, step):
    flips = [order(group, core)[step] for core in (0, 1)]
    return lax.ppermute(value, ALL, [(i, flipped(i, flips[i % 2])) for i in range(128)])


def code_masks(group, core):
    shift = {"z": 4, "x": 2, "y": 0}
    bits = [mask << shift[axis] for axis, mask in order(group, core)]
    return [functools.reduce(lambda a, b: a ^ b, [bits[k] for k in range(6) if r >> k & 1], 0) for r in range(64)]


def swap_cores(value):
    return lax.ppermute(value, "core", [(0, 1), (1, 0)])


def chosen_of(frag_ref, plan_ref):
    current = lax.rem(frag_ref[0], LAYERS)
    return jnp.where(plan_ref[0] == current, 0, jnp.where(plan_ref[1] == current, 1, 2))


def lanes(start, size):
    return pl.ds(pl.multiple_of(start, 128), size)


def outer(anchor, momentum, summed):
    pseudo = summed * 0.5
    momentum_new = outer_mu * momentum + pseudo
    return anchor - outer_rate * (pseudo + outer_mu * momentum_new), momentum_new


def fetch(jobs, sem):
    copies = [
        pltpu.make_async_copy(src.at[(*index, slice(None), lanes(at, PART))], to, sem.at[i])
        for i, (src, index, at, to) in enumerate(jobs)
    ]
    for copy in copies:
        copy.start()
    for copy in copies:
        copy.wait()


OLD = outer_rate * outer_mu * outer_mu
NEW = outer_rate * (1.0 + outer_mu) * 0.5


def first_kernel(
    frag_ref, plan_ref, anchor_ref, momentum_ref, params_ref, same_ref, cross_ref, keep_ref, give_ref, rest_ref, held, sem
):
    island, core, layer = lax.axis_index("yl"), lax.axis_index("core"), chosen_of(frag_ref, plan_ref)
    jobs = []
    for part in (1 - island, island):
        for half in (core, 1 - core):
            at = half * HALF + part * PART
            jobs += [(anchor_ref, (), at, held.at[len(jobs)]), (params_ref, (0, layer), at, held.at[len(jobs) + 1])]
    for half in (core, 1 - core):
        jobs.append((momentum_ref, (), half * HALF + island * PART, held.at[len(jobs)]))
    fetch(jobs, sem)
    same_ref[...] = (held[0] - held[1]).astype(jnp.bfloat16)
    cross_ref[...] = (held[2] - held[3]).astype(jnp.bfloat16)
    for i, (out_ref, half) in enumerate(((keep_ref, core), (give_ref, 1 - core))):
        anchor = held[4 + 2 * i]
        diff = anchor - held[5 + 2 * i]
        out_ref[...] = anchor - OLD * held[8 + i] - NEW * diff
        rest_ref[:, lanes(half * PART, PART)] = diff.astype(jnp.bfloat16)


def join_kernel(keep_ref, got_ref, same_ref, cross_ref, after_ref, *refs):
    outs, rows_ref = refs[:-1], refs[-1]
    core = lax.axis_index("core")
    for at, base_ref, term_ref in ((core, keep_ref, same_ref), (1 - core, got_ref, cross_ref)):
        rows = pl.ds(pl.multiple_of(at * ROWS, 8), ROWS)
        rows_ref[rows, :] = base_ref[...] - NEW * term_ref[...].astype(jnp.float32)
    done = 0
    for q, out_ref in enumerate(outs):
        share = SHARE[q]
        if share < ROOM:
            out_ref[0, CHIP + share : CHIP + ROOM] = jnp.zeros((ROOM - share, TILE), jnp.bfloat16)
        for at, tile, start, size in (
            (0, q, 0, CHIP),
            (CHIP, 2 * GROUPS, done, share),
            (CHIP + ROOM, GROUPS + q, 0, CHIP),
        ):
            value = rows_ref[start : start + size, tile * TILE : (tile + 1) * TILE]
            out_ref[0, at : at + size] = value.astype(jnp.bfloat16)
        done += share


def layers_kernel(
    frag_ref, plan_ref, p_ref, g_ref, m_ref, v_ref, anchor_ref, momentum_ref, same_ref, cross_ref, rest_ref, *refs
):
    p_out, m_out, v_out, momentum_out, done_ref = refs[-5:]
    chosen = pl.program_id(0) == LAYERS - 1

    @pl.when(jnp.logical_not(chosen))
    def _():
        grad = g_ref[...].astype(jnp.float32)
        first = beta_one * m_ref[...] + (1.0 - beta_one) * grad
        second = beta_two * v_ref[...] + (1.0 - beta_two) * grad * grad
        first_hat = first * (1.0 / (1.0 - beta_one**STEP))
        second_hat = second * (1.0 / (1.0 - beta_two**STEP))
        p_out[...] = p_ref[...] * (1.0 - inner_rate * decay_rate) - inner_rate * first_hat / (
            jnp.sqrt(second_hat) + adam_eps
        )
        m_out[...] = first
        v_out[...] = second

    @pl.when(chosen)
    def _():
        core, island = lax.axis_index("core"), lax.axis_index("yl")
        for half in (0, 1):
            for part in (0, 1):
                at = half * HALF + part * PART
                cols = slice(at, at + PART)
                got = jnp.where(
                    half == core, same_ref[...].astype(jnp.float32), cross_ref[...].astype(jnp.float32)
                )
                rest = rest_ref[:, half * PART : (half + 1) * PART].astype(jnp.float32)
                anchor = anchor_ref[:, cols]
                summed = (anchor - p_ref[0, 0, :, cols]).astype(jnp.bfloat16).astype(jnp.float32) + jnp.where(
                    part == island, got, rest
                )
                new, momentum_new = outer(anchor, momentum_ref[:, cols], summed)
                p_out[0, 0, :, cols] = new
                momentum_out[:, cols] = momentum_new
        m_out[...] = m_ref[...]
        v_out[...] = v_ref[...]

    done_ref[...] = jnp.zeros_like(done_ref)


STEP_ROWS = 512


def result_columns(tiles, half):
    return [half * HALF + part * PART + tile * TILE for tile in tiles for part in (0, 1)]


def piece_of(pieces, r, tile, q, size):
    at = CHIP if tile == 2 * GROUPS else 0 if tile < GROUPS else CHIP + ROOM
    return pieces[r // 32].at[r % 32, pl.ds(at, size)]


def multiply_kernel(tiles, n_pieces, has_buffer, mine_ref, theirs_ref, *refs):
    pieces, refs = refs[:n_pieces], refs[n_pieces + 1 + has_buffer :]
    result_ref, out_ref, weight, staged, load_sem, out_sem, result_sem = refs
    core = lax.axis_index("core")
    here = lax.axis_index("z") * 16 + lax.axis_index("x") * 4 + lax.axis_index("yh") * 2 + lax.axis_index("yl")

    def load_weight(g):
        done = 0
        tile = tiles[g]
        for q in (tile % GROUPS,) if tile < 2 * GROUPS else range(GROUPS):
            size = CHIP if tile < 2 * GROUPS else SHARE[q]
            masks = [code_masks(q, c) for c in (0, 1)]
            own = pieces if n_pieces == 2 else pieces[2 * q : 2 * q + 2]
            for r in range(64):
                code = here ^ jnp.where(core == 0, masks[0][r], masks[1][r])
                pltpu.make_async_copy(
                    piece_of(own, r, tile, q, size),
                    weight.at[g, code // 2, pl.ds(done, size), lanes(code % 2 * TILE, TILE)],
                    load_sem.at[g],
                ).start()
            done += SHARE[q]

    for g in range(len(tiles)):
        load_weight(g)
    columns = result_columns(tiles, core)
    for g in range(len(tiles)):
        pltpu.make_async_copy(weight.at[g], weight.at[g], load_sem.at[g]).wait()
        for i, rows_ref in enumerate((theirs_ref, mine_ref)):
            for at in range(0, TOK, STEP_ROWS):
                staged[i, at : at + STEP_ROWS, 2 * TILE * g : 2 * TILE * (g + 1)] = jnp.dot(
                    rows_ref[at : at + STEP_ROWS], weight[g].reshape(D, 2 * TILE), preferred_element_type=jnp.float32
                ).astype(jnp.bfloat16)
        cols = slice(2 * TILE * g, 2 * TILE * (g + 1))
        pltpu.make_async_copy(staged.at[0, :, cols], out_ref.at[:, cols], out_sem).start()
        for k in (2 * g, 2 * g + 1):
            pltpu.make_async_copy(
                staged.at[1, :, k * TILE : (k + 1) * TILE], result_ref.at[:, lanes(columns[k], TILE)], result_sem
            ).start()
    pltpu.make_async_copy(staged.at[0], staged.at[0], out_sem).wait()
    pltpu.make_async_copy(staged.at[1], staged.at[1], result_sem).wait()


TILES = ((0, 3), (2, 5), (1, 4, 6))


def place_kernel(buffer_ref, *refs):
    received, result_ref, sem = refs[:-2], refs[-2], refs[-1]
    half = 1 - lax.axis_index("core")
    copies = []
    for got, tiles in zip(received, TILES):
        for i, at in enumerate(result_columns(tiles, half)):
            copies.append(
                pltpu.make_async_copy(
                    got.at[:, i * TILE : (i + 1) * TILE], result_ref.at[:, lanes(at, TILE)], sem.at[len(copies)]
                )
            )
    for copy in copies:
        copy.start()
    for copy in copies:
        copy.wait()


ANY = pl.BlockSpec(memory_space=pl.ANY)
VMEM = pl.BlockSpec(memory_space=pltpu.VMEM)
SMEM = pl.BlockSpec(memory_space=pltpu.SMEM)
LIMIT = pltpu.CompilerParams(vmem_limit_bytes=24 * 2**20)
FULL = pltpu.CompilerParams(vmem_limit_bytes=60 * 2**20)
SMALL = pltpu.CompilerParams(vmem_limit_bytes=16 * 2**20)


def shape(dims, dtype):
    return jax.ShapeDtypeStruct(dims, dtype)


def cost(flops, moved):
    return pl.CostEstimate(flops=flops, bytes_accessed=moved, transcendentals=0)


def layers_call(scalars, inner, flat, parts, rest, after):
    def layer(i, frag_ref, plan_ref):
        return (0, lax.rem(chosen_of(frag_ref, plan_ref) + 1 + i, LAYERS), 0, 0)

    def whole(dims):
        return pl.BlockSpec(dims, lambda i, *_: (0, 0))

    stepped = pl.BlockSpec((1, 1, ROWS, D), layer)
    state = shape((1, LAYERS, ROWS, D), jnp.float32)
    return pl.pallas_call(
        layers_kernel,
        grid_spec=pltpu.PrefetchScalarGridSpec(
            num_scalar_prefetch=2,
            grid=(LAYERS,),
            in_specs=[stepped] * 4 + [whole((ROWS, D))] * 2 + [whole((ROWS, PART))] * 2 + [whole((ROWS, 2 * PART))] + [ANY] * len(after),
            out_specs=[stepped] * 3 + [whole((ROWS, D)), whole((8, 128))],
        ),
        out_shape=[state] * 3 + [shape((ROWS, D), jnp.float32), shape((8, 128), jnp.int32)],
        compiler_params=LIMIT,
        cost_estimate=cost(20 * LAYERS * ROWS * D, 30 * LAYERS * ROWS * D),
    )(*scalars, *inner, *flat, *parts, rest, *after)


def multiply_call(tiles, tokens, others, pieces, after, buffer):
    width = 2 * TILE * len(tiles)
    args = [tokens, others, *pieces, after] + ([] if buffer is None else [buffer])
    return pl.pallas_call(
        functools.partial(multiply_kernel, tiles, len(pieces), buffer is not None),
        in_specs=[VMEM] * 2 + [ANY] * (len(args) - 2),
        out_specs=[ANY, ANY],
        out_shape=[shape((TOK, D), jnp.bfloat16), shape((TOK, width), jnp.bfloat16)],
        scratch_shapes=[
            pltpu.VMEM((len(tiles), D // CHIP, CHIP, 2 * TILE), jnp.bfloat16),
            pltpu.VMEM((2, TOK, width), jnp.bfloat16),
            pltpu.SemaphoreType.DMA((len(tiles),)),
            pltpu.SemaphoreType.DMA,
            pltpu.SemaphoreType.DMA,
        ],
        input_output_aliases={} if buffer is None else {len(args) - 1: 0},
        compiler_params=LIMIT,
        cost_estimate=cost(2 * 2 * TOK * D * width, 4 * TOK * D + 2 * D * width),
    )(*args)


def body(inner_params, inner_grads, adam_first, adam_second, anchor, momentum, tokens, frag_index, plan):
    f32, bf16 = jnp.float32, jnp.bfloat16
    scalars = (frag_index, plan)
    others = swap_cores(tokens)

    send_same, send_cross, keep, give, rest = pl.pallas_call(
        first_kernel,
        in_specs=[SMEM] * 2 + [ANY] * 3,
        out_specs=[VMEM] * 5,
        out_shape=[shape((ROWS, PART), bf16)] * 2 + [shape((ROWS, PART), f32)] * 2 + [shape((ROWS, 2 * PART), bf16)],
        scratch_shapes=[pltpu.VMEM((10, ROWS, PART), f32), pltpu.SemaphoreType.DMA((10,))],
        compiler_params=FULL,
    )(*scalars, anchor, momentum, inner_params)
    same = lax.ppermute(send_same, "yl", [(0, 1), (1, 0)])
    cross = lax.ppermute(send_cross, ("yl", "core"), [(i, 3 - i) for i in range(4)])
    got = swap_cores(give)
    cur = pl.pallas_call(
        join_kernel,
        in_specs=[VMEM] * 4 + [ANY],
        out_specs=[VMEM] * GROUPS,
        out_shape=[shape((1, 2 * CHIP + ROOM, TILE), bf16)] * GROUPS,
        scratch_shapes=[pltpu.VMEM((CHIP, PART), f32)],
        compiler_params=SMALL,
    )(keep, got, same, cross, others)
    rest_received = lax.ppermute(rest, "yl", [(0, 1), (1, 0)])

    late = rest_received[0, 0] != rest_received[0, 0]

    def doubled(value, step, before):
        out, arrivals = [], []
        for q in range(GROUPS):
            arrived = exchange(value[q], q, step)
            ahead = (arrivals[q - 1] if q else before)[0]
            waits = (ahead != ahead)[None]
            if step == 2 and q == 0:
                waits = waits | late
            out.append(jnp.concatenate([value[q], jnp.where(waits, value[q], arrived)], axis=0))
            arrivals.append(arrived)
        return out, arrivals[1], arrivals[-1]

    before = jnp.zeros((1, 2 * CHIP + ROOM, TILE), bf16)
    for step in range(4):
        cur, before, _ = doubled(cur, step, before)
    both, _, before = doubled(cur, 4, before)
    params_out, first_out, second_out, momentum_out, done = layers_call(
        (frag_index, plan), (inner_params, inner_grads, adam_first, adam_second), (anchor, momentum), (same, swap_cores(cross)),
        rest_received, (before,),
    )
    sixth = [exchange(both[q], q, 5) for q in range(GROUPS)]
    pieces = [[both[q], sixth[q]] for q in range(GROUPS)]
    swapped, result = [], None
    for tiles in TILES:
        needed = pieces[tiles[0]] if len(tiles) == 2 else sum(pieces, [])
        result, out = multiply_call(tiles, tokens, others, needed, done, result)
        swapped.append(swap_cores(out))
    projected = pl.pallas_call(
        place_kernel,
        in_specs=[ANY] + [VMEM] * GROUPS,
        out_specs=ANY,
        out_shape=shape((TOK, D), bf16),
        scratch_shapes=[pltpu.SemaphoreType.DMA((14,))],
        input_output_aliases={0: 0},
        compiler_params=pltpu.CompilerParams(vmem_limit_bytes=4 * 2**20),
    )(result, *swapped)
    return (params_out, first_out, second_out, momentum_out, projected)


def solution(mesh):
    torus = Mesh(np.asarray(mesh.devices).reshape(2, 4, 4, 2, 2), ALL)
    fsdp = ("z", "x", "yh", "core")
    state = P("yl", None, fsdp, None)
    rows = P(fsdp, None)
    tokens = P(ALL, None)
    return jax.shard_map(
        body,
        mesh=torus,
        in_specs=(state, state, state, state, rows, rows, tokens, P(), P()),
        out_specs=(state, state, state, rows, tokens),
        check_vma=False,
    )
```

```python
import functools

import jax
import jax.numpy as jnp
import numpy as np
from jax import lax
from jax.experimental import pallas as pl
from jax.experimental.pallas import tpu as pltpu
from jax.sharding import Mesh
from jax.sharding import PartitionSpec as P

STEP = 40
LAYERS = 3
outer_rate = 0.7
outer_mu = 0.9
inner_rate = 0.01
decay_rate = 0.1
beta_one = 0.9
beta_two = 0.95
adam_eps = 1e-08

ROWS = 56
CHIP = 2 * ROWS
D = 3584
HALF = D // 2
PART = HALF // 2
TILE = 128
GROUPS = 3
SHARE = (48, 32, 32)
ROOM = max(SHARE)
TOK = 512
PITCH = 64

ALL = ("yl", "z", "x", "yh", "core")
CHIPS = ("z", "x", "yh")
FLIPS = (("x", 1), ("y", 1), ("z", 1), ("x", 3), ("y", 3), ("z", 3))


def order(group, core):
    s = (group + 3 * core) % 6
    return FLIPS[s:] + FLIPS[:s]


def flipped(i, flip):
    core, yh, x, z, yl = i % 2, i // 2 % 2, i // 4 % 4, i // 16 % 4, i // 64
    y = yh * 2 + yl
    axis, mask = flip
    x, y, z = (v ^ mask if name == axis else v for name, v in (("x", x), ("y", y), ("z", z)))
    return ((y % 2 * 4 + z) * 4 + x) * 4 + y // 2 * 2 + core


def exchange(value, group, step):
    flips = [order(group, core)[step] for core in (0, 1)]
    return lax.ppermute(value, ALL, [(i, flipped(i, flips[i % 2])) for i in range(128)])


def code_masks(group, core):
    shift = {"z": 4, "x": 2, "y": 0}
    bits = [mask << shift[axis] for axis, mask in order(group, core)]
    return [functools.reduce(lambda a, b: a ^ b, [bits[k] for k in range(6) if r >> k & 1], 0) for r in range(64)]


def swap_cores(value):
    return lax.ppermute(value, "core", [(0, 1), (1, 0)])


def chosen_of(frag_ref, plan_ref):
    current = lax.rem(frag_ref[0], LAYERS)
    return jnp.where(plan_ref[0] == current, 0, jnp.where(plan_ref[1] == current, 1, 2))


def lanes(start, size):
    return pl.ds(pl.multiple_of(start, 128), size)


def outer(anchor, momentum, summed):
    pseudo = summed * 0.5
    momentum_new = outer_mu * momentum + pseudo
    return anchor - outer_rate * (pseudo + outer_mu * momentum_new), momentum_new


def fetch(jobs, sem):
    copies = [
        pltpu.make_async_copy(src.at[(*index, slice(None), lanes(at, PART))], to, sem.at[i])
        for i, (src, index, at, to) in enumerate(jobs)
    ]
    for copy in copies:
        copy.start()
    for copy in copies:
        copy.wait()


OLD = outer_rate * outer_mu * outer_mu
NEW = outer_rate * (1.0 + outer_mu) * 0.5


def first_kernel(
    frag_ref, plan_ref, anchor_ref, momentum_ref, params_ref, same_ref, cross_ref, keep_ref, give_ref, rest_ref, held, sem
):
    island, core, layer = lax.axis_index("yl"), lax.axis_index("core"), chosen_of(frag_ref, plan_ref)
    jobs = []
    for part in (1 - island, island):
        for half in (core, 1 - core):
            at = half * HALF + part * PART
            jobs += [(anchor_ref, (), at, held.at[len(jobs)]), (params_ref, (0, layer), at, held.at[len(jobs) + 1])]
    for half in (core, 1 - core):
        jobs.append((momentum_ref, (), half * HALF + island * PART, held.at[len(jobs)]))
    fetch(jobs, sem)
    same_ref[...] = (held[0] - held[1]).astype(jnp.bfloat16)
    cross_ref[...] = (held[2] - held[3]).astype(jnp.bfloat16)
    for i, (out_ref, half) in enumerate(((keep_ref, core), (give_ref, 1 - core))):
        anchor = held[4 + 2 * i]
        diff = anchor - held[5 + 2 * i]
        out_ref[...] = anchor - OLD * held[8 + i] - NEW * diff
        for tile in range(PART // TILE):
            rows = jnp.concatenate([diff[:, tile * TILE : (tile + 1) * TILE], jnp.zeros((PITCH - ROWS, TILE), jnp.float32)])
            at = pl.multiple_of((half * (PART // TILE) + tile) * PITCH, PITCH)
            rest_ref[pl.ds(at, PITCH), :] = rows.astype(jnp.bfloat16)


def join_kernel(keep_ref, got_ref, same_ref, cross_ref, after_ref, rest_ref, *refs):
    outs, rows_ref = refs[:GROUPS], refs[-1]
    core = lax.axis_index("core")
    for at, base_ref, term_ref in ((core, keep_ref, same_ref), (1 - core, got_ref, cross_ref)):
        rows = pl.ds(pl.multiple_of(at * ROWS, 8), ROWS)
        rows_ref[rows, :] = base_ref[...] - NEW * term_ref[...].astype(jnp.float32)
    done = 0
    for q, out_ref in enumerate(outs):
        share = SHARE[q]
        if share < ROOM:
            out_ref[0, CHIP + share : CHIP + ROOM] = jnp.zeros((ROOM - share, TILE), jnp.bfloat16)
        for at, tile, start, size in (
            (0, q, 0, CHIP),
            (CHIP, 2 * GROUPS, done, share),
            (CHIP + ROOM, GROUPS + q, 0, CHIP),
        ):
            value = rows_ref[start : start + size, tile * TILE : (tile + 1) * TILE]
            out_ref[0, at : at + size] = value.astype(jnp.bfloat16)
        done += share


def layers_kernel(
    frag_ref, plan_ref, p_ref, g_ref, m_ref, v_ref, anchor_ref, momentum_ref, same_ref, cross_ref, rest_ref, *refs
):
    p_out, m_out, v_out, momentum_out, done_ref = refs[-5:]
    chosen = pl.program_id(0) == LAYERS - 1

    @pl.when(jnp.logical_not(chosen))
    def _():
        grad = g_ref[...].astype(jnp.float32)
        first = beta_one * m_ref[...] + (1.0 - beta_one) * grad
        second = beta_two * v_ref[...] + (1.0 - beta_two) * grad * grad
        first_hat = first * (1.0 / (1.0 - beta_one**STEP))
        second_hat = second * (1.0 / (1.0 - beta_two**STEP))
        p_out[...] = p_ref[...] * (1.0 - inner_rate * decay_rate) - inner_rate * first_hat / (
            jnp.sqrt(second_hat) + adam_eps
        )
        m_out[...] = first
        v_out[...] = second

    @pl.when(chosen)
    def _():
        core, island = lax.axis_index("core"), lax.axis_index("yl")
        for half in (0, 1):
            for part in (0, 1):
                at = half * HALF + part * PART
                cols = slice(at, at + PART)
                got = jnp.where(
                    half == core, same_ref[...].astype(jnp.float32), cross_ref[...].astype(jnp.float32)
                )
                first = half * (PART // TILE)
                rest = jnp.concatenate(
                    [
                        rest_ref[(first + tile) * PITCH : (first + tile + 1) * PITCH].astype(jnp.float32)[:ROWS]
                        for tile in range(PART // TILE)
                    ],
                    axis=1,
                )
                anchor = anchor_ref[:, cols]
                summed = (anchor - p_ref[0, 0, :, cols]).astype(jnp.bfloat16).astype(jnp.float32) + jnp.where(
                    part == island, got, rest
                )
                new, momentum_new = outer(anchor, momentum_ref[:, cols], summed)
                p_out[0, 0, :, cols] = new
                momentum_out[:, cols] = momentum_new
        m_out[...] = m_ref[...]
        v_out[...] = v_ref[...]

    done_ref[...] = jnp.zeros_like(done_ref)


STEP_ROWS = 512


def result_columns(tiles, half):
    return [half * HALF + part * PART + tile * TILE for tile in tiles for part in (0, 1)]


def multiply_kernel(tiles, has_buffer, mine_ref, theirs_ref, *refs):
    pieces, refs = refs[: 2 * GROUPS], refs[2 * GROUPS + 1 + has_buffer :]
    result_ref, out_ref, weight, staged, load_sem, out_sem, result_sem = refs
    core = lax.axis_index("core")
    here = lax.axis_index("z") * 16 + lax.axis_index("x") * 4 + lax.axis_index("yh") * 2 + lax.axis_index("yl")

    def load_weight(g):
        done = 0
        tile = tiles[g]
        for q in (tile % GROUPS,) if tile < 2 * GROUPS else range(GROUPS):
            size = CHIP if tile < 2 * GROUPS else SHARE[q]
            masks = [code_masks(q, c) for c in (0, 1)]
            at = 0 if tile < 2 * GROUPS else CHIP
            for r in range(64):
                code = here ^ jnp.where(core == 0, masks[0][r], masks[1][r])
                pltpu.make_async_copy(
                    pieces[2 * q + r // 32].at[r % 32, pl.ds(at, size)],
                    weight.at[g, code // 2, pl.ds(done, size), lanes(code % 2 * TILE, TILE)],
                    load_sem.at[g],
                ).start()
            done += SHARE[q]

    for g in range(len(tiles)):
        load_weight(g)
    columns = result_columns(tiles, core)
    for g in range(len(tiles)):
        pltpu.make_async_copy(weight.at[g], weight.at[g], load_sem.at[g]).wait()
        for i, rows_ref in enumerate((theirs_ref, mine_ref)):
            for at in range(0, TOK, STEP_ROWS):
                staged[i, at : at + STEP_ROWS, 2 * TILE * g : 2 * TILE * (g + 1)] = jnp.dot(
                    rows_ref[at : at + STEP_ROWS], weight[g].reshape(D, 2 * TILE), preferred_element_type=jnp.float32
                ).astype(jnp.bfloat16)
        cols = slice(2 * TILE * g, 2 * TILE * (g + 1))
        pltpu.make_async_copy(staged.at[0, :, cols], out_ref.at[:, cols], out_sem).start()
        for k in (2 * g, 2 * g + 1):
            pltpu.make_async_copy(
                staged.at[1, :, k * TILE : (k + 1) * TILE], result_ref.at[:, lanes(columns[k], TILE)], result_sem
            ).start()
    pltpu.make_async_copy(staged.at[0], staged.at[0], out_sem).wait()
    pltpu.make_async_copy(staged.at[1], staged.at[1], result_sem).wait()


TILES = ((0, 1, 2, 6), (3, 4, 5))


def place_kernel(buffer_ref, *refs):
    received, result_ref, sem = refs[:-2], refs[-2], refs[-1]
    half = 1 - lax.axis_index("core")
    copies = []
    for got, tiles in zip(received, TILES):
        for i, at in enumerate(result_columns(tiles, half)):
            copies.append(
                pltpu.make_async_copy(
                    got.at[:, i * TILE : (i + 1) * TILE], result_ref.at[:, lanes(at, TILE)], sem.at[len(copies)]
                )
            )
    for copy in copies:
        copy.start()
    for copy in copies:
        copy.wait()


ANY = pl.BlockSpec(memory_space=pl.ANY)
VMEM = pl.BlockSpec(memory_space=pltpu.VMEM)
SMEM = pl.BlockSpec(memory_space=pltpu.SMEM)
LIMIT = pltpu.CompilerParams(vmem_limit_bytes=24 * 2**20)
FULL = pltpu.CompilerParams(vmem_limit_bytes=60 * 2**20)
SMALL = pltpu.CompilerParams(vmem_limit_bytes=16 * 2**20)


def shape(dims, dtype):
    return jax.ShapeDtypeStruct(dims, dtype)


def cost(flops, moved):
    return pl.CostEstimate(flops=flops, bytes_accessed=moved, transcendentals=0)


def layers_call(scalars, inner, flat, parts, rest, after):
    def layer(i, frag_ref, plan_ref):
        return (0, lax.rem(chosen_of(frag_ref, plan_ref) + 1 + i, LAYERS), 0, 0)

    def whole(dims):
        return pl.BlockSpec(dims, lambda i, *_: (0, 0))

    stepped = pl.BlockSpec((1, 1, ROWS, D), layer)
    state = shape((1, LAYERS, ROWS, D), jnp.float32)
    return pl.pallas_call(
        layers_kernel,
        grid_spec=pltpu.PrefetchScalarGridSpec(
            num_scalar_prefetch=2,
            grid=(LAYERS,),
            in_specs=[stepped] * 4 + [whole((ROWS, D))] * 2 + [whole((ROWS, PART))] * 2 + [whole((D // 2 // TILE * PITCH, TILE))] + [ANY] * len(after),
            out_specs=[stepped] * 3 + [whole((ROWS, D)), whole((8, 128))],
        ),
        out_shape=[state] * 3 + [shape((ROWS, D), jnp.float32), shape((8, 128), jnp.int32)],
        compiler_params=LIMIT,
        cost_estimate=cost(20 * LAYERS * ROWS * D, 30 * LAYERS * ROWS * D),
    )(*scalars, *inner, *flat, *parts, rest, *after)


def multiply_call(tiles, tokens, others, pieces, after, buffer):
    width = 2 * TILE * len(tiles)
    args = [tokens, others, *pieces, after] + ([] if buffer is None else [buffer])
    return pl.pallas_call(
        functools.partial(multiply_kernel, tiles, buffer is not None),
        in_specs=[VMEM] * 2 + [ANY] * (len(args) - 2),
        out_specs=[ANY, ANY],
        out_shape=[shape((TOK, D), jnp.bfloat16), shape((TOK, width), jnp.bfloat16)],
        scratch_shapes=[
            pltpu.VMEM((len(tiles), D // CHIP, CHIP, 2 * TILE), jnp.bfloat16),
            pltpu.VMEM((2, TOK, width), jnp.bfloat16),
            pltpu.SemaphoreType.DMA((len(tiles),)),
            pltpu.SemaphoreType.DMA,
            pltpu.SemaphoreType.DMA,
        ],
        input_output_aliases={} if buffer is None else {len(args) - 1: 0},
        compiler_params=LIMIT,
        cost_estimate=cost(2 * 2 * TOK * D * width, 4 * TOK * D + 2 * D * width),
    )(*args)


def body(inner_params, inner_grads, adam_first, adam_second, anchor, momentum, tokens, frag_index, plan):
    f32, bf16 = jnp.float32, jnp.bfloat16
    scalars = (frag_index, plan)
    others = swap_cores(tokens)

    send_same, send_cross, keep, give, rest = pl.pallas_call(
        first_kernel,
        in_specs=[SMEM] * 2 + [ANY] * 3,
        out_specs=[VMEM] * 5,
        out_shape=[shape((ROWS, PART), bf16)] * 2 + [shape((ROWS, PART), f32)] * 2 + [shape((D // 2 // TILE * PITCH, TILE), bf16)],
        scratch_shapes=[pltpu.VMEM((10, ROWS, PART), f32), pltpu.SemaphoreType.DMA((10,))],
        compiler_params=FULL,
    )(*scalars, anchor, momentum, inner_params)
    same = lax.ppermute(send_same, "yl", [(0, 1), (1, 0)])
    cross = lax.ppermute(send_cross, ("yl", "core"), [(i, 3 - i) for i in range(4)])
    got = swap_cores(give)
    *cur, rest = pl.pallas_call(
        join_kernel,
        in_specs=[VMEM] * 4 + [ANY] * 2,
        out_specs=[VMEM] * GROUPS + [ANY],
        out_shape=[shape((1, 2 * CHIP + ROOM, TILE), bf16)] * GROUPS + [shape(rest.shape, bf16)],
        input_output_aliases={5: GROUPS},
        scratch_shapes=[pltpu.VMEM((CHIP, PART), f32)],
        compiler_params=SMALL,
    )(keep, got, same, cross, others, rest)
    rest_received = lax.ppermute(rest, "yl", [(0, 1), (1, 0)])

    def doubled(value, step, before):
        out, arrivals = [], []
        for q in range(GROUPS):
            arrived = exchange(value[q], q, step)
            ahead = (arrivals[q - 1] if q else before)[0]
            waits = (ahead != ahead)[None]
            if step == 2 and q == 0:
                late = rest_received[: 2 * CHIP + ROOM]
                waits = waits | (late != late)[None]
            out.append(jnp.concatenate([value[q], jnp.where(waits, value[q], arrived)], axis=0))
            arrivals.append(arrived)
        return out, arrivals[1]

    before = jnp.zeros((1, 2 * CHIP + ROOM, TILE), bf16)
    for step in range(4):
        cur, before = doubled(cur, step, before)
    cut = CHIP + ROOM
    fifth = [exchange(cur[q], q, 4) for q in range(GROUPS)]
    both = [
        [jnp.concatenate([cur[q][:, rows], fifth[q][:, rows]], axis=0) for q in range(GROUPS)]
        for rows in (slice(0, cut), slice(cut, None))
    ]
    params_out, first_out, second_out, momentum_out, done = layers_call(
        (frag_index, plan), (inner_params, inner_grads, adam_first, adam_second), (anchor, momentum), (same, swap_cores(cross)),
        rest_received, (fifth[-1],),
    )
    sixth = [[exchange(value[q], q, 5) for q in range(GROUPS)] for value in both]
    swapped, result = [], None
    for tiles, have, got in zip(TILES, both, sixth):
        pieces = [piece for q in range(GROUPS) for piece in (have[q], got[q])]
        result, out = multiply_call(tiles, tokens, others, pieces, done, result)
        swapped.append(swap_cores(out))
    projected = pl.pallas_call(
        place_kernel,
        in_specs=[ANY] + [VMEM] * len(TILES),
        out_specs=ANY,
        out_shape=shape((TOK, D), bf16),
        scratch_shapes=[pltpu.SemaphoreType.DMA((14,))],
        input_output_aliases={0: 0},
        compiler_params=pltpu.CompilerParams(vmem_limit_bytes=4 * 2**20),
    )(result, *swapped)
    return (params_out, first_out, second_out, momentum_out, projected)


def solution(mesh):
    torus = Mesh(np.asarray(mesh.devices).reshape(2, 4, 4, 2, 2), ALL)
    fsdp = ("z", "x", "yh", "core")
    state = P("yl", None, fsdp, None)
    rows = P(fsdp, None)
    tokens = P(ALL, None)
    return jax.shard_map(
        body,
        mesh=torus,
        in_specs=(state, state, state, state, rows, rows, tokens, P(), P()),
        out_specs=(state, state, state, rows, tokens),
        check_vma=False,
    )
```

```python
import functools

import jax
import jax.numpy as jnp
import numpy as np
from jax import lax
from jax.experimental import pallas as pl
from jax.experimental.pallas import tpu as pltpu
from jax.sharding import Mesh
from jax.sharding import PartitionSpec as P

STEP = 40
LAYERS = 3
outer_rate = 0.7
outer_mu = 0.9
inner_rate = 0.01
decay_rate = 0.1
beta_one = 0.9
beta_two = 0.95
adam_eps = 1e-08

ROWS = 56
CHIP = 2 * ROWS
D = 3584
HALF = D // 2
PART = HALF // 2
TILE = 128
GROUPS = 3
SHARE = (32, 48, 32)
TOK = 512
PITCH = 64

ALL = ("yl", "z", "x", "yh", "core")
CHIPS = ("z", "x", "yh")
FLIPS = (("x", 1), ("y", 1), ("z", 1), ("x", 3), ("y", 3), ("z", 3))


def order(group, core):
    s = (group + 3 * core) % 6
    return FLIPS[s:] + FLIPS[:s]


def flipped(i, flip):
    core, yh, x, z, yl = i % 2, i // 2 % 2, i // 4 % 4, i // 16 % 4, i // 64
    y = yh * 2 + yl
    axis, mask = flip
    x, y, z = (v ^ mask if name == axis else v for name, v in (("x", x), ("y", y), ("z", z)))
    return ((y % 2 * 4 + z) * 4 + x) * 4 + y // 2 * 2 + core


def exchange(value, group, step):
    flips = [order(group, core)[step] for core in (0, 1)]
    return lax.ppermute(value, ALL, [(i, flipped(i, flips[i % 2])) for i in range(128)])


def code_masks(group, core):
    shift = {"z": 4, "x": 2, "y": 0}
    bits = [mask << shift[axis] for axis, mask in order(group, core)]
    return [functools.reduce(lambda a, b: a ^ b, [bits[k] for k in range(6) if r >> k & 1], 0) for r in range(64)]


def swap_cores(value):
    return lax.ppermute(value, "core", [(0, 1), (1, 0)])


def chosen_of(frag_ref, plan_ref):
    current = lax.rem(frag_ref[0], LAYERS)
    return jnp.where(plan_ref[0] == current, 0, jnp.where(plan_ref[1] == current, 1, 2))


def lanes(start, size):
    return pl.ds(pl.multiple_of(start, 128), size)


def outer(anchor, momentum, summed):
    pseudo = summed * 0.5
    momentum_new = outer_mu * momentum + pseudo
    return anchor - outer_rate * (pseudo + outer_mu * momentum_new), momentum_new


def fetch(jobs, sem):
    copies = [
        pltpu.make_async_copy(src.at[(*index, slice(None), lanes(at, PART))], to, sem.at[i])
        for i, (src, index, at, to) in enumerate(jobs)
    ]
    for copy in copies:
        copy.start()
    for copy in copies:
        copy.wait()


OLD = outer_rate * outer_mu * outer_mu
NEW = outer_rate * (1.0 + outer_mu) * 0.5


def first_kernel(
    frag_ref, plan_ref, anchor_ref, momentum_ref, params_ref, same_ref, cross_ref, keep_ref, give_ref, rest_ref, held, sem
):
    island, core, layer = lax.axis_index("yl"), lax.axis_index("core"), chosen_of(frag_ref, plan_ref)
    jobs = []
    for part in (1 - island, island):
        for half in (core, 1 - core):
            at = half * HALF + part * PART
            jobs += [(anchor_ref, (), at, held.at[len(jobs)]), (params_ref, (0, layer), at, held.at[len(jobs) + 1])]
    for half in (core, 1 - core):
        jobs.append((momentum_ref, (), half * HALF + island * PART, held.at[len(jobs)]))
    fetch(jobs, sem)
    same_ref[...] = (held[0] - held[1]).astype(jnp.bfloat16)
    cross_ref[...] = (held[2] - held[3]).astype(jnp.bfloat16)
    for i, (out_ref, half) in enumerate(((keep_ref, core), (give_ref, 1 - core))):
        anchor = held[4 + 2 * i]
        diff = anchor - held[5 + 2 * i]
        out_ref[...] = anchor - OLD * held[8 + i] - NEW * diff
        for tile in range(PART // TILE):
            rows = jnp.concatenate([diff[:, tile * TILE : (tile + 1) * TILE], jnp.zeros((PITCH - ROWS, TILE), jnp.float32)])
            at = pl.multiple_of((half * (PART // TILE) + tile) * PITCH, PITCH)
            rest_ref[pl.ds(at, PITCH), :] = rows.astype(jnp.bfloat16)


def join_kernel(keep_hbm, got_ref, same_ref, cross_ref, after_ref, rest_ref, *refs):
    outs, (rows_ref, keep_ref, sem) = refs[:GROUPS], refs[-3:]
    core = lax.axis_index("core")
    copy = pltpu.make_async_copy(keep_hbm, keep_ref, sem)
    copy.start()
    for at, base_ref, term_ref in ((1 - core, got_ref, cross_ref), (core, keep_ref, same_ref)):
        if base_ref is keep_ref:
            copy.wait()
        rows = pl.ds(pl.multiple_of(at * ROWS, 8), ROWS)
        rows_ref[rows, :] = base_ref[...] - NEW * term_ref[...].astype(jnp.float32)
    done = 0
    for q, out_ref in enumerate(outs):
        share = SHARE[q]
        for at, tile, start, size in (
            (0, q, 0, CHIP),
            (CHIP, 2 * GROUPS, done, share),
            (CHIP + share, GROUPS + q, 0, CHIP),
        ):
            value = rows_ref[start : start + size, tile * TILE : (tile + 1) * TILE]
            out_ref[0, at : at + size] = value.astype(jnp.bfloat16)
        done += share


def layers_kernel(
    frag_ref, plan_ref, p_ref, g_ref, m_ref, v_ref, anchor_ref, momentum_ref, same_ref, cross_ref, rest_ref, *refs
):
    p_out, m_out, v_out, momentum_out, done_ref = refs[-5:]
    chosen = pl.program_id(0) == LAYERS - 1

    @pl.when(jnp.logical_not(chosen))
    def _():
        grad = g_ref[...].astype(jnp.float32)
        first = beta_one * m_ref[...] + (1.0 - beta_one) * grad
        second = beta_two * v_ref[...] + (1.0 - beta_two) * grad * grad
        first_hat = first * (1.0 / (1.0 - beta_one**STEP))
        second_hat = second * (1.0 / (1.0 - beta_two**STEP))
        p_out[...] = p_ref[...] * (1.0 - inner_rate * decay_rate) - inner_rate * first_hat / (
            jnp.sqrt(second_hat) + adam_eps
        )
        m_out[...] = first
        v_out[...] = second

    @pl.when(chosen)
    def _():
        core, island = lax.axis_index("core"), lax.axis_index("yl")
        for half in (0, 1):
            for part in (0, 1):
                at = half * HALF + part * PART
                cols = slice(at, at + PART)
                got = jnp.where(
                    half == core, same_ref[...].astype(jnp.float32), cross_ref[...].astype(jnp.float32)
                )
                first = half * (PART // TILE)
                rest = jnp.concatenate(
                    [
                        rest_ref[(first + tile) * PITCH : (first + tile + 1) * PITCH].astype(jnp.float32)[:ROWS]
                        for tile in range(PART // TILE)
                    ],
                    axis=1,
                )
                anchor = anchor_ref[:, cols]
                summed = (anchor - p_ref[0, 0, :, cols]).astype(jnp.bfloat16).astype(jnp.float32) + jnp.where(
                    part == island, got, rest
                )
                new, momentum_new = outer(anchor, momentum_ref[:, cols], summed)
                p_out[0, 0, :, cols] = new
                momentum_out[:, cols] = momentum_new
        m_out[...] = m_ref[...]
        v_out[...] = v_ref[...]

    done_ref[...] = jnp.zeros_like(done_ref)


STEP_ROWS = 512


def result_columns(tiles, half):
    return [half * HALF + part * PART + tile * TILE for tile in tiles for part in (0, 1)]


def multiply_kernel(tiles, has_buffer, mine_ref, theirs_ref, *refs):
    pieces, refs = refs[: 2 * GROUPS], refs[2 * GROUPS + 1 + has_buffer :]
    result_ref, out_ref, weight, staged, load_sem, out_sem, result_sem = refs
    core = lax.axis_index("core")
    here = lax.axis_index("z") * 16 + lax.axis_index("x") * 4 + lax.axis_index("yh") * 2 + lax.axis_index("yl")

    def load_weight(g):
        done = 0
        tile = tiles[g]
        for q in (tile % GROUPS,) if tile < 2 * GROUPS else range(GROUPS):
            size = CHIP if tile < 2 * GROUPS else SHARE[q]
            masks = [code_masks(q, c) for c in (0, 1)]
            at = 0 if tile < 2 * GROUPS else CHIP
            for r in range(64):
                code = here ^ jnp.where(core == 0, masks[0][r], masks[1][r])
                pltpu.make_async_copy(
                    pieces[2 * q + r // 32].at[r % 32, pl.ds(at, size)],
                    weight.at[g, code // 2, pl.ds(done, size), lanes(code % 2 * TILE, TILE)],
                    load_sem.at[g],
                ).start()
            done += SHARE[q]

    for g in range(len(tiles)):
        load_weight(g)
    columns = result_columns(tiles, core)
    for g in range(len(tiles)):
        pltpu.make_async_copy(weight.at[g], weight.at[g], load_sem.at[g]).wait()
        for i, rows_ref in enumerate((theirs_ref, mine_ref)):
            for at in range(0, TOK, STEP_ROWS):
                staged[i, at : at + STEP_ROWS, 2 * TILE * g : 2 * TILE * (g + 1)] = jnp.dot(
                    rows_ref[at : at + STEP_ROWS], weight[g].reshape(D, 2 * TILE), preferred_element_type=jnp.float32
                ).astype(jnp.bfloat16)
        cols = slice(2 * TILE * g, 2 * TILE * (g + 1))
        pltpu.make_async_copy(staged.at[0, :, cols], out_ref.at[:, cols], out_sem).start()
        for k in (2 * g, 2 * g + 1):
            pltpu.make_async_copy(
                staged.at[1, :, k * TILE : (k + 1) * TILE], result_ref.at[:, lanes(columns[k], TILE)], result_sem
            ).start()
    pltpu.make_async_copy(staged.at[0], staged.at[0], out_sem).wait()
    pltpu.make_async_copy(staged.at[1], staged.at[1], result_sem).wait()


TILES = ((0, 1, 2, 6), (3, 4, 5))


def place_kernel(buffer_ref, *refs):
    received, result_ref, sem = refs[:-2], refs[-2], refs[-1]
    half = 1 - lax.axis_index("core")
    copies = []
    for got, tiles in zip(received, TILES):
        for i, at in enumerate(result_columns(tiles, half)):
            copies.append(
                pltpu.make_async_copy(
                    got.at[:, i * TILE : (i + 1) * TILE], result_ref.at[:, lanes(at, TILE)], sem.at[len(copies)]
                )
            )
    for copy in copies:
        copy.start()
    for copy in copies:
        copy.wait()


ANY = pl.BlockSpec(memory_space=pl.ANY)
VMEM = pl.BlockSpec(memory_space=pltpu.VMEM)
SMEM = pl.BlockSpec(memory_space=pltpu.SMEM)
HBM = pl.BlockSpec(memory_space=pltpu.HBM)
LIMIT = pltpu.CompilerParams(vmem_limit_bytes=24 * 2**20)
FULL = pltpu.CompilerParams(vmem_limit_bytes=60 * 2**20)
SMALL = pltpu.CompilerParams(vmem_limit_bytes=16 * 2**20)


def shape(dims, dtype):
    return jax.ShapeDtypeStruct(dims, dtype)


def cost(flops, moved):
    return pl.CostEstimate(flops=flops, bytes_accessed=moved, transcendentals=0)


def layers_call(scalars, inner, flat, parts, rest, after):
    def layer(i, frag_ref, plan_ref):
        return (0, lax.rem(chosen_of(frag_ref, plan_ref) + 1 + i, LAYERS), 0, 0)

    def whole(dims):
        return pl.BlockSpec(dims, lambda i, *_: (0, 0))

    stepped = pl.BlockSpec((1, 1, ROWS, D), layer)
    state = shape((1, LAYERS, ROWS, D), jnp.float32)
    return pl.pallas_call(
        layers_kernel,
        grid_spec=pltpu.PrefetchScalarGridSpec(
            num_scalar_prefetch=2,
            grid=(LAYERS,),
            in_specs=[stepped] * 4 + [whole((ROWS, D))] * 2 + [whole((ROWS, PART))] * 2 + [whole((D // 2 // TILE * PITCH, TILE))] + [ANY] * len(after),
            out_specs=[stepped] * 3 + [whole((ROWS, D)), whole((8, 128))],
        ),
        out_shape=[state] * 3 + [shape((ROWS, D), jnp.float32), shape((8, 128), jnp.int32)],
        compiler_params=LIMIT,
        cost_estimate=cost(20 * LAYERS * ROWS * D, 30 * LAYERS * ROWS * D),
    )(*scalars, *inner, *flat, *parts, rest, *after)


def multiply_call(tiles, tokens, others, pieces, after, buffer):
    width = 2 * TILE * len(tiles)
    args = [tokens, others, *pieces, after] + ([] if buffer is None else [buffer])
    return pl.pallas_call(
        functools.partial(multiply_kernel, tiles, buffer is not None),
        in_specs=[VMEM] * 2 + [ANY] * (len(args) - 2),
        out_specs=[ANY, ANY],
        out_shape=[shape((TOK, D), jnp.bfloat16), shape((TOK, width), jnp.bfloat16)],
        scratch_shapes=[
            pltpu.VMEM((len(tiles), D // CHIP, CHIP, 2 * TILE), jnp.bfloat16),
            pltpu.VMEM((2, TOK, width), jnp.bfloat16),
            pltpu.SemaphoreType.DMA((len(tiles),)),
            pltpu.SemaphoreType.DMA,
            pltpu.SemaphoreType.DMA,
        ],
        input_output_aliases={} if buffer is None else {len(args) - 1: 0},
        compiler_params=LIMIT,
        cost_estimate=cost(2 * 2 * TOK * D * width, 4 * TOK * D + 2 * D * width),
    )(*args)


def body(inner_params, inner_grads, adam_first, adam_second, anchor, momentum, tokens, frag_index, plan):
    f32, bf16 = jnp.float32, jnp.bfloat16
    scalars = (frag_index, plan)
    others = swap_cores(tokens)

    send_same, send_cross, keep, give, rest = pl.pallas_call(
        first_kernel,
        in_specs=[SMEM] * 2 + [ANY] * 3,
        out_specs=[VMEM] * 5,
        out_shape=[shape((ROWS, PART), bf16)] * 2 + [shape((ROWS, PART), f32)] * 2 + [shape((D // 2 // TILE * PITCH, TILE), bf16)],
        scratch_shapes=[pltpu.VMEM((10, ROWS, PART), f32), pltpu.SemaphoreType.DMA((10,))],
        compiler_params=FULL,
    )(*scalars, anchor, momentum, inner_params)
    same = lax.ppermute(send_same, "yl", [(0, 1), (1, 0)])
    cross = lax.ppermute(send_cross, ("yl", "core"), [(i, 3 - i) for i in range(4)])
    got = swap_cores(give)
    *cur, rest = pl.pallas_call(
        join_kernel,
        in_specs=[HBM] + [VMEM] * 3 + [ANY, HBM],
        out_specs=[VMEM] * GROUPS + [HBM],
        out_shape=[shape((1, 2 * CHIP + share, TILE), bf16) for share in SHARE] + [shape(rest.shape, bf16)],
        input_output_aliases={5: GROUPS},
        scratch_shapes=[pltpu.VMEM((CHIP, PART), f32), pltpu.VMEM((ROWS, PART), f32), pltpu.SemaphoreType.DMA],
        compiler_params=SMALL,
    )(keep, got, same, cross, others, rest)
    rest_received = lax.ppermute(rest, "yl", [(0, 1), (1, 0)])

    def differs(held, like):
        rows = min(held.shape[0], like.shape[1])
        return jnp.pad(held[:rows] != held[:rows], ((0, like.shape[1] - rows), (0, 0)))[None]

    def doubled(value, step, before):
        out, arrivals = [], []
        for q in range(GROUPS):
            arrived = exchange(value[q], q, step)
            ahead = (arrivals[q - 1] if q else before)[0]
            waits = differs(ahead, value[q])
            if step == 2 and q == 0:
                waits = waits | differs(rest_received, value[q])
            out.append(jnp.concatenate([value[q], jnp.where(waits, value[q], arrived)], axis=0))
            arrivals.append(arrived)
        return out, arrivals[1]

    before = jnp.zeros((1, CHIP, TILE), bf16)
    for step in range(4):
        cur, before = doubled(cur, step, before)
    fifth = [exchange(cur[q], q, 4) for q in range(GROUPS)]
    both = [
        [jnp.concatenate([cur[q][:, rows(q)], fifth[q][:, rows(q)]], axis=0) for q in range(GROUPS)]
        for rows in (lambda q: slice(0, CHIP + SHARE[q]), lambda q: slice(CHIP + SHARE[q], None))
    ]
    params_out, first_out, second_out, momentum_out, done = layers_call(
        (frag_index, plan), (inner_params, inner_grads, adam_first, adam_second), (anchor, momentum), (same, swap_cores(cross)),
        rest_received, (fifth[-1],),
    )
    sixth = [[exchange(value[q], q, 5) for q in range(GROUPS)] for value in both]
    swapped, result = [], None
    for tiles, have, got in zip(TILES, both, sixth):
        pieces = [piece for q in range(GROUPS) for piece in (have[q], got[q])]
        result, out = multiply_call(tiles, tokens, others, pieces, done, result)
        swapped.append(swap_cores(out))
    projected = pl.pallas_call(
        place_kernel,
        in_specs=[ANY] + [VMEM] * len(TILES),
        out_specs=ANY,
        out_shape=shape((TOK, D), bf16),
        scratch_shapes=[pltpu.SemaphoreType.DMA((14,))],
        input_output_aliases={0: 0},
        compiler_params=pltpu.CompilerParams(vmem_limit_bytes=4 * 2**20),
    )(result, *swapped)
    return (params_out, first_out, second_out, momentum_out, projected)


def solution(mesh):
    torus = Mesh(np.asarray(mesh.devices).reshape(2, 4, 4, 2, 2), ALL)
    fsdp = ("z", "x", "yh", "core")
    state = P("yl", None, fsdp, None)
    rows = P(fsdp, None)
    tokens = P(ALL, None)
    return jax.shard_map(
        body,
        mesh=torus,
        in_specs=(state, state, state, state, rows, rows, tokens, P(), P()),
        out_specs=(state, state, state, rows, tokens),
        check_vma=False,
    )
```

```python
import functools

import jax
import jax.numpy as jnp
import numpy as np
from jax import lax
from jax.experimental import pallas as pl
from jax.experimental.pallas import tpu as pltpu
from jax.sharding import Mesh
from jax.sharding import PartitionSpec as P

STEP = 40
LAYERS = 3
outer_rate = 0.7
outer_mu = 0.9
inner_rate = 0.01
decay_rate = 0.1
beta_one = 0.9
beta_two = 0.95
adam_eps = 1e-08

ROWS = 56
CHIP = 2 * ROWS
D = 3584
HALF = D // 2
PART = HALF // 2
TILE = 128
GROUPS = 3
SHARE = (32, 48, 32)
TOK = 512
PITCH = 64

ALL = ("yl", "z", "x", "yh", "core")
CHIPS = ("z", "x", "yh")
FLIPS = (("x", 1), ("y", 1), ("z", 1), ("x", 3), ("y", 3), ("z", 3))


def order(group, core):
    s = (group + 3 * core) % 6
    return FLIPS[s:] + FLIPS[:s]


def flipped(i, flip):
    core, yh, x, z, yl = i % 2, i // 2 % 2, i // 4 % 4, i // 16 % 4, i // 64
    y = yh * 2 + yl
    axis, mask = flip
    x, y, z = (v ^ mask if name == axis else v for name, v in (("x", x), ("y", y), ("z", z)))
    return ((y % 2 * 4 + z) * 4 + x) * 4 + y // 2 * 2 + core


def exchange(value, group, step):
    flips = [order(group, core)[step] for core in (0, 1)]
    return lax.ppermute(value, ALL, [(i, flipped(i, flips[i % 2])) for i in range(128)])


def code_masks(group, core):
    shift = {"z": 4, "x": 2, "y": 0}
    bits = [mask << shift[axis] for axis, mask in order(group, core)]
    return [functools.reduce(lambda a, b: a ^ b, [bits[k] for k in range(6) if r >> k & 1], 0) for r in range(64)]


def swap_cores(value):
    return lax.ppermute(value, "core", [(0, 1), (1, 0)])


def chosen_of(frag_ref, plan_ref):
    current = lax.rem(frag_ref[0], LAYERS)
    return jnp.where(plan_ref[0] == current, 0, jnp.where(plan_ref[1] == current, 1, 2))


def lanes(start, size):
    return pl.ds(pl.multiple_of(start, 128), size)


def outer(anchor, momentum, summed):
    pseudo = summed * 0.5
    momentum_new = outer_mu * momentum + pseudo
    return anchor - outer_rate * (pseudo + outer_mu * momentum_new), momentum_new


def fetch(jobs, sem):
    copies = [
        pltpu.make_async_copy(src.at[(*index, slice(None), lanes(at, PART))], to, sem.at[i])
        for i, (src, index, at, to) in enumerate(jobs)
    ]
    for copy in copies:
        copy.start()
    for copy in copies:
        copy.wait()


OLD = outer_rate * outer_mu * outer_mu
NEW = outer_rate * (1.0 + outer_mu) * 0.5


def first_kernel(
    frag_ref, plan_ref, anchor_ref, momentum_ref, params_ref, same_ref, cross_ref, keep_ref, give_ref, rest_ref, held, sem
):
    island, core, layer = lax.axis_index("yl"), lax.axis_index("core"), chosen_of(frag_ref, plan_ref)
    jobs = []
    for part in (1 - island, island):
        for half in (core, 1 - core):
            at = half * HALF + part * PART
            jobs += [(anchor_ref, (), at, held.at[len(jobs)]), (params_ref, (0, layer), at, held.at[len(jobs) + 1])]
    for half in (core, 1 - core):
        jobs.append((momentum_ref, (), half * HALF + island * PART, held.at[len(jobs)]))
    fetch(jobs, sem)
    same_ref[...] = (held[0] - held[1]).astype(jnp.bfloat16)
    cross_ref[...] = (held[2] - held[3]).astype(jnp.bfloat16)
    for i, (out_ref, half) in enumerate(((keep_ref, core), (give_ref, 1 - core))):
        anchor = held[4 + 2 * i]
        diff = anchor - held[5 + 2 * i]
        out_ref[...] = anchor - OLD * held[8 + i] - NEW * diff
        for tile in range(PART // TILE):
            rows = jnp.concatenate([diff[:, tile * TILE : (tile + 1) * TILE], jnp.zeros((PITCH - ROWS, TILE), jnp.float32)])
            at = pl.multiple_of((half * (PART // TILE) + tile) * PITCH, PITCH)
            rest_ref[pl.ds(at, PITCH), :] = rows.astype(jnp.bfloat16)


def join_kernel(keep_hbm, got_ref, same_ref, cross_ref, after_ref, rest_ref, *refs):
    outs, (rows_ref, keep_ref, sem) = refs[:GROUPS], refs[-3:]
    core = lax.axis_index("core")
    copy = pltpu.make_async_copy(keep_hbm, keep_ref, sem)
    copy.start()
    for at, base_ref, term_ref in ((1 - core, got_ref, cross_ref), (core, keep_ref, same_ref)):
        if base_ref is keep_ref:
            copy.wait()
        rows = pl.ds(pl.multiple_of(at * ROWS, 8), ROWS)
        rows_ref[rows, :] = base_ref[...] - NEW * term_ref[...].astype(jnp.float32)
    done = 0
    for q, out_ref in enumerate(outs):
        share = SHARE[q]
        for at, tile, start, size in (
            (0, q, 0, CHIP),
            (CHIP, 2 * GROUPS, done, share),
            (CHIP + share, GROUPS + q, 0, CHIP),
        ):
            value = rows_ref[start : start + size, tile * TILE : (tile + 1) * TILE]
            out_ref[0, at : at + size] = value.astype(jnp.bfloat16)
        done += share


def layers_kernel(
    frag_ref, plan_ref, p_ref, g_ref, m_ref, v_ref, anchor_ref, momentum_ref, same_ref, cross_ref, rest_ref, *refs
):
    p_out, m_out, v_out, momentum_out, done_ref = refs[-5:]
    chosen = pl.program_id(0) == LAYERS - 1

    @pl.when(jnp.logical_not(chosen))
    def _():
        grad = g_ref[...].astype(jnp.float32)
        first = beta_one * m_ref[...] + (1.0 - beta_one) * grad
        second = beta_two * v_ref[...] + (1.0 - beta_two) * grad * grad
        first_hat = first * (1.0 / (1.0 - beta_one**STEP))
        second_hat = second * (1.0 / (1.0 - beta_two**STEP))
        p_out[...] = p_ref[...] * (1.0 - inner_rate * decay_rate) - inner_rate * first_hat / (
            jnp.sqrt(second_hat) + adam_eps
        )
        m_out[...] = first
        v_out[...] = second

    @pl.when(chosen)
    def _():
        core, island = lax.axis_index("core"), lax.axis_index("yl")
        for half in (0, 1):
            for part in (0, 1):
                at = half * HALF + part * PART
                cols = slice(at, at + PART)
                got = jnp.where(
                    half == core, same_ref[...].astype(jnp.float32), cross_ref[...].astype(jnp.float32)
                )
                first = half * (PART // TILE)
                rest = jnp.concatenate(
                    [
                        rest_ref[(first + tile) * PITCH : (first + tile + 1) * PITCH].astype(jnp.float32)[:ROWS]
                        for tile in range(PART // TILE)
                    ],
                    axis=1,
                )
                anchor = anchor_ref[:, cols]
                summed = (anchor - p_ref[0, 0, :, cols]).astype(jnp.bfloat16).astype(jnp.float32) + jnp.where(
                    part == island, got, rest
                )
                new, momentum_new = outer(anchor, momentum_ref[:, cols], summed)
                p_out[0, 0, :, cols] = new
                momentum_out[:, cols] = momentum_new
        m_out[...] = m_ref[...]
        v_out[...] = v_ref[...]

    done_ref[...] = jnp.zeros_like(done_ref)


STEP_ROWS = 512


def result_columns(tiles, half):
    return [half * HALF + part * PART + tile * TILE for tile in tiles for part in (0, 1)]


def multiply_kernel(tiles, has_buffer, mine_ref, theirs_ref, *refs):
    pieces, refs = refs[: 2 * GROUPS], refs[2 * GROUPS + 1 + has_buffer :]
    result_ref, out_ref, weight, staged, load_sem, out_sem, result_sem = refs
    core = lax.axis_index("core")
    here = lax.axis_index("z") * 16 + lax.axis_index("x") * 4 + lax.axis_index("yh") * 2 + lax.axis_index("yl")

    def load_weight(g):
        done = 0
        tile = tiles[g]
        for q in (tile % GROUPS,) if tile < 2 * GROUPS else range(GROUPS):
            size = CHIP if tile < 2 * GROUPS else SHARE[q]
            masks = [code_masks(q, c) for c in (0, 1)]
            at = SHARE[tile % GROUPS] if GROUPS <= tile < 2 * GROUPS else 0
            for r in range(64):
                code = here ^ jnp.where(core == 0, masks[0][r], masks[1][r])
                pltpu.make_async_copy(
                    pieces[2 * q + r // 32].at[r % 32, pl.ds(at, size)],
                    weight.at[g, code // 2, pl.ds(done, size), lanes(code % 2 * TILE, TILE)],
                    load_sem.at[g],
                ).start()
            done += SHARE[q]

    for g in range(len(tiles)):
        load_weight(g)
    columns = result_columns(tiles, core)
    for g in range(len(tiles)):
        pltpu.make_async_copy(weight.at[g], weight.at[g], load_sem.at[g]).wait()
        for i, rows_ref in enumerate((theirs_ref, mine_ref)):
            for at in range(0, TOK, STEP_ROWS):
                staged[i, at : at + STEP_ROWS, 2 * TILE * g : 2 * TILE * (g + 1)] = jnp.dot(
                    rows_ref[at : at + STEP_ROWS], weight[g].reshape(D, 2 * TILE), preferred_element_type=jnp.float32
                ).astype(jnp.bfloat16)
        cols = slice(2 * TILE * g, 2 * TILE * (g + 1))
        pltpu.make_async_copy(staged.at[0, :, cols], out_ref.at[:, cols], out_sem).start()
        for k in (2 * g, 2 * g + 1):
            pltpu.make_async_copy(
                staged.at[1, :, k * TILE : (k + 1) * TILE], result_ref.at[:, lanes(columns[k], TILE)], result_sem
            ).start()
    pltpu.make_async_copy(staged.at[0], staged.at[0], out_sem).wait()
    pltpu.make_async_copy(staged.at[1], staged.at[1], result_sem).wait()


TILES = ((0, 1, 2), (3, 4, 5, 6))


def place_kernel(buffer_ref, *refs):
    received, result_ref, sem = refs[:-2], refs[-2], refs[-1]
    half = 1 - lax.axis_index("core")
    copies = []
    for got, tiles in zip(received, TILES):
        for i, at in enumerate(result_columns(tiles, half)):
            copies.append(
                pltpu.make_async_copy(
                    got.at[:, i * TILE : (i + 1) * TILE], result_ref.at[:, lanes(at, TILE)], sem.at[len(copies)]
                )
            )
    for copy in copies:
        copy.start()
    for copy in copies:
        copy.wait()


ANY = pl.BlockSpec(memory_space=pl.ANY)
VMEM = pl.BlockSpec(memory_space=pltpu.VMEM)
SMEM = pl.BlockSpec(memory_space=pltpu.SMEM)
HBM = pl.BlockSpec(memory_space=pltpu.HBM)
LIMIT = pltpu.CompilerParams(vmem_limit_bytes=24 * 2**20)
FULL = pltpu.CompilerParams(vmem_limit_bytes=60 * 2**20)
SMALL = pltpu.CompilerParams(vmem_limit_bytes=16 * 2**20)


def shape(dims, dtype):
    return jax.ShapeDtypeStruct(dims, dtype)


def cost(flops, moved):
    return pl.CostEstimate(flops=flops, bytes_accessed=moved, transcendentals=0)


def layers_call(scalars, inner, flat, parts, rest, after):
    def layer(i, frag_ref, plan_ref):
        return (0, lax.rem(chosen_of(frag_ref, plan_ref) + 1 + i, LAYERS), 0, 0)

    def whole(dims):
        return pl.BlockSpec(dims, lambda i, *_: (0, 0))

    stepped = pl.BlockSpec((1, 1, ROWS, D), layer)
    state = shape((1, LAYERS, ROWS, D), jnp.float32)
    return pl.pallas_call(
        layers_kernel,
        grid_spec=pltpu.PrefetchScalarGridSpec(
            num_scalar_prefetch=2,
            grid=(LAYERS,),
            in_specs=[stepped] * 4 + [whole((ROWS, D))] * 2 + [whole((ROWS, PART))] * 2 + [whole((D // 2 // TILE * PITCH, TILE))] + [ANY] * len(after),
            out_specs=[stepped] * 3 + [whole((ROWS, D)), whole((8, 128))],
        ),
        out_shape=[state] * 3 + [shape((ROWS, D), jnp.float32), shape((8, 128), jnp.int32)],
        compiler_params=LIMIT,
        cost_estimate=cost(20 * LAYERS * ROWS * D, 30 * LAYERS * ROWS * D),
    )(*scalars, *inner, *flat, *parts, rest, *after)


def multiply_call(tiles, tokens, others, pieces, after, buffer):
    width = 2 * TILE * len(tiles)
    args = [tokens, others, *pieces, after] + ([] if buffer is None else [buffer])
    return pl.pallas_call(
        functools.partial(multiply_kernel, tiles, buffer is not None),
        in_specs=[VMEM] * 2 + [ANY] * (len(args) - 2),
        out_specs=[ANY, ANY],
        out_shape=[shape((TOK, D), jnp.bfloat16), shape((TOK, width), jnp.bfloat16)],
        scratch_shapes=[
            pltpu.VMEM((len(tiles), D // CHIP, CHIP, 2 * TILE), jnp.bfloat16),
            pltpu.VMEM((2, TOK, width), jnp.bfloat16),
            pltpu.SemaphoreType.DMA((len(tiles),)),
            pltpu.SemaphoreType.DMA,
            pltpu.SemaphoreType.DMA,
        ],
        input_output_aliases={} if buffer is None else {len(args) - 1: 0},
        compiler_params=LIMIT,
        cost_estimate=cost(2 * 2 * TOK * D * width, 4 * TOK * D + 2 * D * width),
    )(*args)


def body(inner_params, inner_grads, adam_first, adam_second, anchor, momentum, tokens, frag_index, plan):
    f32, bf16 = jnp.float32, jnp.bfloat16
    scalars = (frag_index, plan)
    others = swap_cores(tokens)

    send_same, send_cross, keep, give, rest = pl.pallas_call(
        first_kernel,
        in_specs=[SMEM] * 2 + [ANY] * 3,
        out_specs=[VMEM] * 5,
        out_shape=[shape((ROWS, PART), bf16)] * 2 + [shape((ROWS, PART), f32)] * 2 + [shape((D // 2 // TILE * PITCH, TILE), bf16)],
        scratch_shapes=[pltpu.VMEM((10, ROWS, PART), f32), pltpu.SemaphoreType.DMA((10,))],
        compiler_params=FULL,
    )(*scalars, anchor, momentum, inner_params)
    same = lax.ppermute(send_same, "yl", [(0, 1), (1, 0)])
    cross = lax.ppermute(send_cross, ("yl", "core"), [(i, 3 - i) for i in range(4)])
    got = swap_cores(give)
    *cur, rest = pl.pallas_call(
        join_kernel,
        in_specs=[HBM] + [VMEM] * 3 + [ANY, HBM],
        out_specs=[VMEM] * GROUPS + [HBM],
        out_shape=[shape((1, 2 * CHIP + share, TILE), bf16) for share in SHARE] + [shape(rest.shape, bf16)],
        input_output_aliases={5: GROUPS},
        scratch_shapes=[pltpu.VMEM((CHIP, PART), f32), pltpu.VMEM((ROWS, PART), f32), pltpu.SemaphoreType.DMA],
        compiler_params=SMALL,
    )(keep, got, same, cross, others, rest)
    rest_received = lax.ppermute(rest, "yl", [(0, 1), (1, 0)])

    def differs(held, like):
        rows = min(held.shape[0], like.shape[1])
        return jnp.pad(held[:rows] != held[:rows], ((0, like.shape[1] - rows), (0, 0)))[None]

    def doubled(value, step, before):
        out, arrivals = [], []
        for q in range(GROUPS):
            arrived = exchange(value[q], q, step)
            ahead = (arrivals[q - 1] if q else before)[0]
            waits = differs(ahead, value[q])
            if step == 2 and q == 0:
                waits = waits | differs(rest_received, value[q])
            out.append(jnp.concatenate([value[q], jnp.where(waits, value[q], arrived)], axis=0))
            arrivals.append(arrived)
        return out, arrivals[1]

    before = jnp.zeros((1, CHIP, TILE), bf16)
    for step in range(4):
        cur, before = doubled(cur, step, before)
    fifth = [exchange(cur[q], q, 4) for q in range(GROUPS)]
    both = [
        [jnp.concatenate([cur[q][:, rows(q)], fifth[q][:, rows(q)]], axis=0) for q in range(GROUPS)]
        for rows in (lambda q: slice(0, CHIP), lambda q: slice(CHIP, None))
    ]
    params_out, first_out, second_out, momentum_out, done = layers_call(
        (frag_index, plan), (inner_params, inner_grads, adam_first, adam_second), (anchor, momentum), (same, swap_cores(cross)),
        rest_received, (fifth[-1],),
    )
    sixth = [[exchange(value[q], q, 5) for q in range(GROUPS)] for value in both]
    swapped, result = [], None
    for tiles, have, got in zip(TILES, both, sixth):
        pieces = [piece for q in range(GROUPS) for piece in (have[q], got[q])]
        result, out = multiply_call(tiles, tokens, others, pieces, done, result)
        swapped.append(swap_cores(out))
    projected = pl.pallas_call(
        place_kernel,
        in_specs=[ANY] + [VMEM] * len(TILES),
        out_specs=ANY,
        out_shape=shape((TOK, D), bf16),
        scratch_shapes=[pltpu.SemaphoreType.DMA((14,))],
        input_output_aliases={0: 0},
        compiler_params=pltpu.CompilerParams(vmem_limit_bytes=4 * 2**20),
    )(result, *swapped)
    return (params_out, first_out, second_out, momentum_out, projected)


def solution(mesh):
    torus = Mesh(np.asarray(mesh.devices).reshape(2, 4, 4, 2, 2), ALL)
    fsdp = ("z", "x", "yh", "core")
    state = P("yl", None, fsdp, None)
    rows = P(fsdp, None)
    tokens = P(ALL, None)
    return jax.shard_map(
        body,
        mesh=torus,
        in_specs=(state, state, state, state, rows, rows, tokens, P(), P()),
        out_specs=(state, state, state, rows, tokens),
        check_vma=False,
    )
```
